32 devices in a mesh: dp: 8 (over z, core), expert: 4 (over y, x).
Axes of the slice: x: 2, y: 2, z: 4, core: 2. Of those that a mesh axis runs over, the one named last changes fastest.
Arguments:
- tokens: bfloat16 [4096, 4096], P(('dp', 'expert')), may hold values from -6 to 6
- expert_ids: int32 [4096, 2], P(('dp', 'expert')), may hold values from 0 to 3, all different within a row; in each aligned block of 128 rows (0 to 127, 128 to 255, ...) at most 80 rows name the same one
- gate_probs: float32 [4096, 2], P(('dp', 'expert')), may hold values from 0.2 to 1
- gate_weight: bfloat16 [4, 4096, 1536], P('expert', 'dp'), may hold values from -0.09375 to 0.09375
- up_weight: bfloat16 [4, 4096, 1536], P('expert', 'dp'), may hold values from -0.09375 to 0.09375
- down_weight: bfloat16 [4, 1536, 4096], P('expert', None, 'dp'), may hold values from -0.15625 to 0.15625
Outputs:
- mixed: bfloat16 [4096, 4096], P(('dp', 'expert'))
The draws below stay inside these ranges and needn't reach their ends.
Inputs may be any that keep to these rules, and one draw needn't show every extreme that they name: `expert_ids`: each token names 2 different experts. Among the 128 tokens of one device (aligned blocks of rows), no expert is named by more than 80 tokens, and in every draw some expert is named by exactly 80 tokens of some device.
All inputs are finite; a program needn't handle non-finite values.
Results may differ from the reference program's by a relative error of at most 0.0057.
Values may be sent and summed in bfloat16 or wider, within the bound.
No kernel may reach another device: no remote copies, remote signals or barrier semaphores. Data moves between devices by JAX's collectives and lax.ppermute only.
A program may use at most 128 MiB of HBM per device.

```python
import math
import jax
import jax.numpy as jnp
import numpy as np
from jax import lax

D = 4096
FF = 1536
TOP = 2
TOK_DEV = 128
EXPERTS = 4
CAP = 80
TOKENS = 4096
N_DP = 8
N_EXPERT = 4


def levels(own_key, dims, split, low, high):
    def one(dim, parts):
        heights = jax.random.uniform(jax.random.fold_in(jax.random.fold_in(own_key, 6), dim), (parts,), jnp.float32, low / len(split), high / len(split))
        return jnp.repeat(jnp.exp(heights), dims[dim] // parts).reshape((-1,) + (1,) * (len(dims) - dim - 1))

    factor_of = one(*split[0])
    for cut in split[1:]:
        factor_of = factor_of * one(*cut)
    return factor_of


def routed_block(key, own, number, rows, number_of, top, most, slope):
    sequence = jax.random.permutation(key, number_of)
    packed, usual = shares(number_of, rows * top, most, slope, True), shares(number_of, rows * top, most, slope, False)
    places = jnp.arange(number_of)

    def named(sizes, offset_by):
        used = int((sizes > 0).sum())
        fixed = max(1, used // 4)
        shifted = fixed + (places - fixed + offset_by * (used - fixed)) % max(1, number_of - fixed)
        return jnp.zeros((number_of,), jnp.int32).at[sequence[jnp.where(places < fixed, places, shifted)]].set(jnp.asarray(sizes, jnp.int32))

    sizes = jnp.where(number % 4 == 0, named(packed, number // 4), named(usual, number - number // 4 - 1))
    mixed = jax.random.permutation(jax.random.fold_in(own, 3), number_of)
    donor, sink = mixed[0:number_of // 2 * 2:2], mixed[1:number_of // 2 * 2:2]
    slack = jnp.minimum(sizes[donor] - 1, most - sizes[sink]) // 2
    slack = jnp.where((donor == sequence[0]) | (sink == sequence[0]) | (sizes[sink] == 0), 0, jnp.maximum(slack, 0))
    shifted = jax.random.randint(jax.random.fold_in(own, 4), (number_of // 2,), 0, 1 << 20) % (slack + 1)
    sizes = sizes.at[donor].add(-shifted).at[sink].add(shifted)
    labels = jnp.searchsorted(jnp.cumsum(sizes), jnp.arange(rows * top), side="right").astype(jnp.int32)
    grid = labels.reshape(top, rows).T
    grid = grid[jax.random.permutation(jax.random.fold_in(own, 1), rows)]
    offset_by = jax.random.randint(jax.random.fold_in(own, 2), (rows, 1), 0, top)
    return jnp.take_along_axis(grid, (jnp.arange(top)[None, :] + offset_by) % top, axis=1)


def shares(number_of, total, limit, skew, full):
    loads = [(1 << 20) // math.isqrt(standing ** skew) + 1 for standing in range(1, number_of + 1)]
    largest = limit if full else min(limit, max(-(-total // number_of), total * loads[0] // sum(loads)))
    least = 1 if total - largest >= number_of - 1 else 0
    holding, surplus = [largest] + [least] * (number_of - 1), total - largest - least * (number_of - 1)
    while surplus > 0:
        candidates = [i for i in range(1, number_of) if holding[i] < largest] or [i for i in range(1, number_of) if holding[i] < limit]
        pool, budget = sum([loads[i] for i in candidates]), surplus
        for i in candidates:
            extra = min(limit - holding[i], max(1, budget * loads[i] // pool), surplus)
            holding[i] = holding[i] + extra
            surplus = surplus - extra
    return np.array(holding)


def noise(key, shape, spread, limit, shards=(), kind=jnp.bfloat16):
    array = jax.random.normal(key, shape, jnp.float32) * spread
    if len(shards) > 0:
        array = levels(key, shape, shards, -0.22, 0.18) * array
    return jnp.clip(array, min=-limit, max=limit).astype(kind)


def setup_inputs(seed: int = 0) -> dict:
    key_list = jax.random.split(jax.random.key(seed), 7)
    tokens = noise(key_list[0], (TOKENS, D), 1.0, 6.0, ((0, 32),))
    expert_ids_keys = jax.random.split(jax.random.fold_in(key_list[1], 1), TOKENS // TOK_DEV)
    expert_ids_turns = jax.random.permutation(jax.random.fold_in(key_list[1], 3), TOKENS // TOK_DEV)
    expert_ids = jax.vmap(lambda own, number: routed_block(jax.random.fold_in(key_list[1], 2), own, number, TOK_DEV, EXPERTS, TOP, CAP, 2))(expert_ids_keys, expert_ids_turns).reshape((TOKENS, TOP))
    gate_probs = jnp.clip(0.2 + 0.8 * jax.random.uniform(key_list[2], (TOKENS, TOP), jnp.float32) ** levels(key_list[2], (TOKENS, TOP), ((0, 32),), -0.2, 0.2), 0.2, 1.0)
    gate_weight = noise(key_list[3], (EXPERTS, D, FF), D ** -0.5, 0.09375, ((0, 4), (1, 8)))
    up_weight = noise(key_list[4], (EXPERTS, D, FF), D ** -0.5, 0.09375, ((0, 4), (1, 8)))
    down_weight = noise(key_list[5], (EXPERTS, FF, D), FF ** -0.5, 0.15625, ((0, 4), (2, 8)))
    return dict(tokens=tokens, expert_ids=expert_ids, gate_probs=gate_probs, gate_weight=gate_weight, up_weight=up_weight, down_weight=down_weight)


def reference(tokens, expert_ids, gate_probs, gate_weight, up_weight, down_weight):
    tok_count = tokens.shape[0]
    top_count = expert_ids.shape[1]
    flat_ids = expert_ids.reshape(-1).astype(jnp.int32)
    flat_probs = gate_probs.reshape(-1)
    ordering = jnp.argsort(flat_ids, stable=True).astype(jnp.int32)
    expert_range = jnp.arange(EXPERTS, dtype=jnp.int32)
    tallies = jnp.sum((flat_ids[:, None] == expert_range[None, :]).astype(jnp.int32), axis=0).astype(jnp.int32)
    beginnings = (jnp.cumsum(tallies) - tallies).astype(jnp.int32)
    window = N_DP * N_EXPERT * CAP
    row_block = math.gcd(window, 512)
    block_count = window // row_block
    padded_order = jnp.concatenate([ordering, jnp.zeros((window,), jnp.int32)])

    def per_expert(mixed, expert):
        def per_block(mixed, block_index):
            def compute(mixed):
                first = (beginnings[expert] + block_index * row_block).astype(jnp.int32)
                picked = lax.dynamic_slice(padded_order, (first,), (row_block,))
                valid = block_index * row_block + jnp.arange(row_block, dtype=jnp.int32) < tallies[expert]
                token_rows = (picked // top_count).astype(jnp.int32)
                rows = tokens[token_rows]
                gate = jnp.dot(rows, gate_weight[expert], preferred_element_type=jnp.float32)
                upper = jnp.dot(rows, up_weight[expert], preferred_element_type=jnp.float32)
                hidden = (jax.nn.silu(gate) * upper).astype(jnp.bfloat16)
                outputs = jnp.dot(hidden, down_weight[expert], preferred_element_type=jnp.float32).astype(jnp.bfloat16)
                scale = jnp.where(valid, flat_probs[picked], jnp.zeros_like(flat_probs[picked]))
                return mixed.at[token_rows].add(scale[:, None] * outputs.astype(jnp.float32))
            return lax.cond(block_index * row_block < tallies[expert], compute, lambda unchanged: unchanged, mixed), None
        mixed, unused = lax.scan(per_block, mixed, jnp.arange(block_count, dtype=jnp.int32))
        return mixed, None

    mixed, unused = lax.scan(per_expert, jnp.zeros((tok_count, tokens.shape[1]), jnp.float32), expert_range)
    return mixed.astype(jnp.bfloat16)
```

```python
import jax
import jax.numpy as jnp
from jax import lax
from jax.sharding import PartitionSpec as P

CAP = 80
F32 = jnp.float32
BF16 = jnp.bfloat16
NOTE_ROWS = 8


def ranks_of(ids, groups):
    flat = ids.reshape(-1)
    count = flat.shape[0]
    onehot = (flat[:, None] == jnp.arange(groups, dtype=jnp.int32)).astype(BF16)
    before = (jnp.arange(count)[:, None] > jnp.arange(count)[None, :]).astype(BF16)
    ranks = jnp.dot(before, onehot, preferred_element_type=F32)
    return jnp.sum(ranks * onehot.astype(F32), axis=1).reshape(ids.shape)


def take(array, index):
    return lax.dynamic_index_in_dim(array, index, 0, keepdims=False)


def on_device(tokens, expert_ids, gate_probs, gate_weight, up_weight, down_weight):
    tok_count, model_width = tokens.shape
    top = expert_ids.shape[1]
    n_dp, groups = lax.axis_size("dp"), lax.axis_size("expert")
    planes = n_dp // 2
    place = lax.axis_index("dp")
    plane, core = place // 2, place % 2
    width = model_width // n_dp
    hidden_width = gate_weight.shape[2]
    half = hidden_width // 2
    slots = groups * CAP
    swap = [(i, i ^ 1) for i in range(n_dp)]

    def other(array):
        return lax.ppermute(array, "dp", swap)

    def columns(array, which):
        return lax.dynamic_slice_in_dim(array, which * half, half, 1)

    def split(array):
        return [take(array, which) for which in range(array.shape[0])]

    notes = jnp.concatenate([expert_ids.astype(F32).T, ranks_of(expert_ids, groups).T], axis=0)
    notes = jnp.pad(notes, ((0, NOTE_ROWS - 2 * top), (0, width - tok_count))).astype(BF16)
    sent = jnp.concatenate([tokens, jnp.tile(notes, (1, n_dp))], axis=0)
    arrived = lax.all_to_all(sent, "dp", split_axis=1, concat_axis=0, tiled=True)
    arrived = arrived.reshape(n_dp, tok_count + NOTE_ROWS, width)

    gate_local, up_local, down_local = gate_weight[0], up_weight[0], down_weight[0]
    keep = jnp.concatenate([columns(gate_local, core), columns(up_local, core)], axis=1)
    give = jnp.concatenate([columns(gate_local, 1 - core), columns(up_local, 1 - core)], axis=1)
    in_weight = jnp.concatenate([keep, other(give)], axis=0)
    other_probs = other(gate_probs)
    probs = jnp.where(core == 0, jnp.stack([gate_probs, other_probs]), jnp.stack([other_probs, gate_probs]))
    arrived, in_weight, probs, down_local = lax.optimization_barrier((arrived, in_weight, probs, down_local))

    told = arrived[:, tok_count : tok_count + 2 * top, :tok_count].astype(jnp.int32)
    slot = (told[:, :top] ^ lax.axis_index("expert")) * CAP + told[:, top:]
    slot_range = jnp.arange(slots, dtype=jnp.int32)[:, None]

    def across(blocks):
        return [blocks[0]] + [
            lax.ppermute(blocks[k], "expert", [(i, i ^ k) for i in range(groups)]) for k in range(1, groups)
        ]

    def routed(first, count):
        tokens_there = lax.dynamic_slice_in_dim(arrived[:, :tok_count], 2 * first, 2 * count, 0)
        slot_there = lax.dynamic_slice_in_dim(slot, 2 * first, 2 * count, 0)
        chosen = sum((slot_there[:, k, None, :] == slot_range).astype(BF16) for k in range(top))
        sending = jnp.einsum("dst,dtc->dsc", chosen, tokens_there, preferred_element_type=F32).astype(BF16)
        sending = sending.reshape(2 * count, groups, CAP, width)
        rows = jnp.concatenate(across([sending[:, k] for k in range(groups)]), axis=1)
        rows = rows.reshape(2 * count * slots, width)
        return jnp.concatenate([rows, other(rows)], axis=1).reshape(count, 2, slots, 2 * width)

    mid = planes // 2
    rising = plane < mid
    far_first = jnp.where(rising, mid, 0)
    near_first = mid - far_first
    far_rows = routed(far_first, planes - mid)

    def pass_on(below, above, step):
        upward = [(2 * i + c, 2 * i + 2 + c) for i in range(step - 1, planes - 1) for c in (0, 1)]
        downward = [(2 * i + 2 + c, 2 * i + c) for i in range(planes - step) for c in (0, 1)]
        return lax.ppermute(below, "dp", upward), lax.ppermute(above, "dp", downward)

    def product(rows):
        return jnp.dot(rows, in_weight, preferred_element_type=F32)

    def rows_for(far, near, target, side):
        there = (target >= mid) == rising
        return jnp.where(there, take(far[:, side], target % mid), take(near[:, side], target % mid))

    def add_on(far, near, side, below, above, step):
        upward = [(2 * i + c, 2 * i + 2 + c) for i in range(step) for c in (0, 1)]
        downward = [(2 * (planes - 1 - i) + c, 2 * (planes - 2 - i) + c) for i in range(step) for c in (0, 1)]
        if step <= mid:
            target = jnp.where(rising, plane - step, plane + step) % planes
            send = product(take(far[:, side], target % mid))
            if below is not None:
                send = send + jnp.where(rising, below, above).astype(F32)
            going_up = going_down = send.astype(BF16)
        else:
            going_up = product(rows_for(far, near, (plane - step) % planes, side))
            going_down = product(rows_for(far, near, (plane + step) % planes, side))
            going_up = (going_up + below.astype(F32)).astype(BF16)
            going_down = (going_down + above.astype(F32)).astype(BF16)
        return lax.ppermute(going_up, "dp", upward), lax.ppermute(going_down, "dp", downward)

    passed = [(down_local, down_local)]
    passed.append(pass_on(*passed[0], 1))
    near_rows = routed(near_first, mid)
    sums = [(None, None), (None, None)]
    for step in range(1, planes):
        sums[0] = add_on(far_rows, near_rows, 0, *sums[0], step)
        far_rows, sums[1], passed[step] = lax.optimization_barrier((far_rows, sums[1], passed[step]))
        if step == mid:
            far_rows, near_rows = lax.optimization_barrier((far_rows, near_rows))
        if step + 1 < planes:
            passed.append(pass_on(*passed[step], step + 1))
        sums[1] = add_on(far_rows, near_rows, 1, *sums[1], step)
    pieces = [down_local] + [
        jnp.where(plane >= step, passed[step][0], passed[planes - step][1]) for step in range(1, planes)
    ]
    pieces = jnp.stack(pieces)
    out_weight = jnp.concatenate([take(pieces, (plane - p) % planes) for p in range(planes)], axis=1)
    out_weight, near_rows = lax.optimization_barrier((out_weight, near_rows))

    def returned(side):
        below, above = sums[side]
        total = product(take(near_rows[:, side], plane % mid)) + below.astype(F32) + above.astype(F32)
        hidden = (jax.nn.silu(total[:, :half]) * total[:, half:]).astype(BF16)
        apart = other(hidden)
        hidden = jnp.concatenate(
            [jnp.where(core == 0, hidden, apart), jnp.where(core == 0, apart, hidden)], axis=1
        )
        return jnp.dot(hidden, out_weight, preferred_element_type=F32).astype(BF16).reshape(groups, CAP, -1)

    def combined(side, blocks):
        back = jnp.concatenate(across(split(blocks)), axis=0)
        side_slot = take(slot, 2 * plane + side)
        coarse = lax.reduce_precision(probs[side], 8, 7)
        weights = [
            sum(jnp.where(side_slot[k, :, None] == slot_range[:, 0], part[:, k, None], 0.0) for k in range(top)).astype(BF16)
            for part in (coarse, probs[side] - coarse)
        ]
        both = jnp.dot(jnp.concatenate(weights, axis=0), back, preferred_element_type=F32)
        return (both[:tok_count] + both[tok_count:]).astype(BF16)

    first = returned(0)
    first, sums[1] = lax.optimization_barrier((first, sums[1]))
    mixed = [combined(0, first), combined(1, returned(1))]
    mine = jnp.where(core == 0, mixed[0], mixed[1])
    theirs = other(jnp.where(core == 0, mixed[1], mixed[0]))
    sides = [jnp.where(core == 0, mine, theirs), jnp.where(core == 0, theirs, mine)]
    sides = [side.reshape(tok_count, planes, width) for side in sides]
    return jnp.stack(sides, axis=2).reshape(tok_count, model_width)


def solution(mesh):
    placed = (
        P(("dp", "expert"), None),
        P(("dp", "expert"), None),
        P(("dp", "expert"), None),
        P("expert", "dp", None),
        P("expert", "dp", None),
        P("expert", None, "dp"),
    )
    return jax.shard_map(
        on_device, mesh=mesh, in_specs=placed, out_specs=P(("dp", "expert"), None), check_vma=False
    )
```

```python
import jax
import jax.numpy as jnp
from jax import lax
from jax.sharding import PartitionSpec as P

CAP = 80
F32 = jnp.float32
BF16 = jnp.bfloat16
NOTE_ROWS = 8


def ranks_of(ids, groups):
    flat = ids.reshape(-1)
    count = flat.shape[0]
    onehot = (flat[:, None] == jnp.arange(groups, dtype=jnp.int32)).astype(BF16)
    before = (jnp.arange(count)[:, None] > jnp.arange(count)[None, :]).astype(BF16)
    ranks = jnp.dot(before, onehot, preferred_element_type=F32)
    return jnp.sum(ranks * onehot.astype(F32), axis=1).reshape(ids.shape)


def take(array, index):
    return lax.dynamic_index_in_dim(array, index, 0, keepdims=False)


def on_device(tokens, expert_ids, gate_probs, gate_weight, up_weight, down_weight):
    tok_count, model_width = tokens.shape
    top = expert_ids.shape[1]
    n_dp, groups = lax.axis_size("dp"), lax.axis_size("expert")
    planes = n_dp // 2
    place = lax.axis_index("dp")
    plane, core = place // 2, place % 2
    width = model_width // n_dp
    hidden_width = gate_weight.shape[2]
    half = hidden_width // 2
    slots = groups * CAP
    swap = [(i, i ^ 1) for i in range(n_dp)]

    def other(array):
        return lax.ppermute(array, "dp", swap)

    def columns(array, which):
        return lax.dynamic_slice_in_dim(array, which * half, half, 1)

    def split(array):
        return [take(array, which) for which in range(array.shape[0])]

    notes = jnp.concatenate([expert_ids.astype(F32).T, ranks_of(expert_ids, groups).T], axis=0)
    notes = jnp.pad(notes, ((0, NOTE_ROWS - 2 * top), (0, width - tok_count))).astype(BF16)
    sent = jnp.concatenate([tokens, jnp.tile(notes, (1, n_dp))], axis=0)
    arrived = lax.all_to_all(sent, "dp", split_axis=1, concat_axis=0, tiled=True)
    arrived = arrived.reshape(n_dp, tok_count + NOTE_ROWS, width)

    gate_local, up_local, down_local = gate_weight[0], up_weight[0], down_weight[0]
    keep = jnp.concatenate([columns(gate_local, core), columns(up_local, core)], axis=1)
    give = jnp.concatenate([columns(gate_local, 1 - core), columns(up_local, 1 - core)], axis=1)
    in_weight = jnp.concatenate([keep, other(give)], axis=0)
    other_probs = other(gate_probs)
    probs = jnp.where(core == 0, jnp.stack([gate_probs, other_probs]), jnp.stack([other_probs, gate_probs]))
    arrived, in_weight, probs, down_local = lax.optimization_barrier((arrived, in_weight, probs, down_local))

    told = arrived[:, tok_count : tok_count + 2 * top, :tok_count].astype(jnp.int32)
    slot = (told[:, :top] ^ lax.axis_index("expert")) * CAP + told[:, top:]
    slot_range = jnp.arange(slots, dtype=jnp.int32)[:, None]

    def across(blocks):
        return [blocks[0]] + [
            lax.ppermute(blocks[k], "expert", [(i, i ^ k) for i in range(groups)]) for k in range(1, groups)
        ]

    def pass_on(below, above, step):
        upward = [(2 * i + c, 2 * i + 2 + c) for i in range(step - 1, planes - 1) for c in (0, 1)]
        downward = [(2 * i + 2 + c, 2 * i + c) for i in range(planes - step) for c in (0, 1)]
        return lax.ppermute(below, "dp", upward), lax.ppermute(above, "dp", downward)

    passed = [(down_local, down_local)]
    passed.append(pass_on(*passed[0], 1))

    chosen = sum((slot[:, k, None, :] == slot_range).astype(BF16) for k in range(top))
    sending = jnp.einsum("dst,dtc->dsc", chosen, arrived[:, :tok_count], preferred_element_type=F32).astype(BF16)
    sending = sending.reshape(n_dp, groups, CAP, width)
    rows = jnp.concatenate(across([sending[:, k] for k in range(groups)]), axis=1)
    rows = rows.reshape(planes, 2 * slots, width)
    rows, passed[1] = lax.optimization_barrier((rows, passed[1]))

    def whole(first, count):
        some = lax.dynamic_slice_in_dim(rows, first, count, 0)
        return jnp.concatenate([some, other(some)], axis=2).reshape(count, 2, slots, 2 * width)

    def together(*values):
        return lax.optimization_barrier(values)

    mid = planes // 2
    rising = plane < mid
    far_first = jnp.where(rising, mid, 0)
    near_first = mid - far_first
    far = whole(far_first, planes - mid)

    def product(rows):
        return jnp.dot(rows, in_weight, preferred_element_type=F32)

    def add_on(side, below, above, step):
        if step <= mid:
            target = jnp.where(rising, plane - step, plane + step) % planes
            send = product(take(far[:, side], target % mid))
            if below is not None:
                send = send + jnp.where(rising, below, above).astype(F32)
            return send.astype(BF16), send.astype(BF16)
        sending = []
        for target, so_far in (((plane - step) % planes, below), ((plane + step) % planes, above)):
            there = (target >= mid) == rising
            rows = jnp.where(there, take(far[:, side], target % mid), take(near[:, side], target % mid))
            sending.append((product(rows) + so_far.astype(F32)).astype(BF16))
        return tuple(sending)

    def send_on(sending, step):
        upward = [(2 * i + c, 2 * i + 2 + c) for i in range(step) for c in (0, 1)]
        downward = [(2 * (planes - 1 - i) + c, 2 * (planes - 2 - i) + c) for i in range(step) for c in (0, 1)]
        if step == 1:
            both = lax.ppermute(sending[0], "dp", upward + downward)
            return both, both
        return lax.ppermute(sending[0], "dp", upward), lax.ppermute(sending[1], "dp", downward)

    near = whole(near_first, mid)
    sums = [(None, None), (None, None)]
    for step in range(1, planes):
        sums[0] = send_on(add_on(0, *sums[0], step), step)
        if step > 1:
            far, sums[1], passed[step] = together(far, sums[1], passed[step])
        if step + 1 < planes:
            passed.append(pass_on(*passed[step], step + 1))
        sending = add_on(1, *sums[1], step)
        _, sums[0] = together(sending, sums[0])
        sums[1] = send_on(sending, step)
    pieces = [down_local] + [
        jnp.where(plane >= step, passed[step][0], passed[planes - step][1]) for step in range(1, planes)
    ]
    pieces = jnp.stack(pieces)
    out_weight = jnp.concatenate([take(pieces, (plane - p) % planes) for p in range(planes)], axis=1)

    def returned(side):
        total = product(take(near[:, side], plane % mid))
        below, above = sums[side]
        total = total + below.astype(F32) + above.astype(F32)
        hidden = (jax.nn.silu(total[:, :half]) * total[:, half:]).astype(BF16)
        apart = other(hidden)
        hidden = jnp.concatenate(
            [jnp.where(core == 0, hidden, apart), jnp.where(core == 0, apart, hidden)], axis=1
        )
        outputs = jnp.dot(hidden, out_weight, preferred_element_type=F32).astype(BF16).reshape(groups, CAP, -1)
        return jnp.concatenate(across(split(outputs)), axis=0)

    def combined(side, back):
        side_slot = take(slot, 2 * plane + side)
        coarse = lax.reduce_precision(probs[side], 8, 7)
        weights = [
            sum(jnp.where(side_slot[k, :, None] == slot_range[:, 0], part[:, k, None], 0.0) for k in range(top)).astype(BF16)
            for part in (coarse, probs[side] - coarse)
        ]
        both = jnp.dot(jnp.concatenate(weights, axis=0), back, preferred_element_type=F32)
        return (both[:tok_count] + both[tok_count:]).astype(BF16)

    first = returned(0)
    first, sums[1] = together(first, sums[1])
    mixed = [combined(0, first), combined(1, returned(1))]
    mine = jnp.where(core == 0, mixed[0], mixed[1])
    theirs = other(jnp.where(core == 0, mixed[1], mixed[0]))
    sides = [jnp.where(core == 0, mine, theirs), jnp.where(core == 0, theirs, mine)]
    return jnp.concatenate(
        [side[:, p * width : (p + 1) * width] for p in range(planes) for side in sides], axis=1
    )


def solution(mesh):
    placed = (
        P(("dp", "expert"), None),
        P(("dp", "expert"), None),
        P(("dp", "expert"), None),
        P("expert", "dp", None),
        P("expert", "dp", None),
        P("expert", None, "dp"),
    )
    return jax.shard_map(
        on_device, mesh=mesh, in_specs=placed, out_specs=P(("dp", "expert"), None), check_vma=False
    )
```

```python
import jax
import jax.numpy as jnp
from jax import lax
from jax.sharding import PartitionSpec as P

CAP = 80
PARTS = ((0, 40), (40, 80))
F32 = jnp.float32
BF16 = jnp.bfloat16
NOTE_ROWS = 8


def ranks_of(ids, groups):
    flat = ids.reshape(-1)
    count = flat.shape[0]
    onehot = (flat[:, None] == jnp.arange(groups, dtype=jnp.int32)).astype(BF16)
    before = (jnp.arange(count)[:, None] > jnp.arange(count)[None, :]).astype(BF16)
    ranks = jnp.dot(before, onehot, preferred_element_type=F32)
    return jnp.sum(ranks * onehot.astype(F32), axis=1).reshape(ids.shape)


def take(array, index):
    return lax.dynamic_index_in_dim(array, index, 0, keepdims=False)


def on_device(tokens, expert_ids, gate_probs, gate_weight, up_weight, down_weight):
    tok_count, model_width = tokens.shape
    top = expert_ids.shape[1]
    n_dp, groups = lax.axis_size("dp"), lax.axis_size("expert")
    planes = n_dp // 2
    place = lax.axis_index("dp")
    plane, core = place // 2, place % 2
    width = model_width // n_dp
    hidden_width = gate_weight.shape[2]
    half = hidden_width // 2
    slots = groups * CAP
    swap = [(i, i ^ 1) for i in range(n_dp)]

    def other(array):
        return lax.ppermute(array, "dp", swap)

    def columns(array, which):
        return lax.dynamic_slice_in_dim(array, which * half, half, 1)

    def split(array):
        return [take(array, which) for which in range(array.shape[0])]

    notes = jnp.concatenate([expert_ids.astype(F32).T, ranks_of(expert_ids, groups).T], axis=0)
    notes = jnp.pad(notes, ((0, NOTE_ROWS - 2 * top), (0, width - tok_count))).astype(BF16)
    sent = jnp.concatenate([tokens, jnp.tile(notes, (1, n_dp))], axis=0)
    arrived = lax.all_to_all(sent, "dp", split_axis=1, concat_axis=0, tiled=True)
    arrived = arrived.reshape(n_dp, tok_count + NOTE_ROWS, width)

    gate_local, up_local, down_local = gate_weight[0], up_weight[0], down_weight[0]
    keep = jnp.concatenate([columns(gate_local, core), columns(up_local, core)], axis=1)
    give = jnp.concatenate([columns(gate_local, 1 - core), columns(up_local, 1 - core)], axis=1)
    in_weight = jnp.concatenate([keep, other(give)], axis=0)
    other_probs = other(gate_probs)
    probs = jnp.where(core == 0, jnp.stack([gate_probs, other_probs]), jnp.stack([other_probs, gate_probs]))
    arrived, in_weight, probs = lax.optimization_barrier((arrived, in_weight, probs))

    told = arrived[:, tok_count : tok_count + 2 * top, :tok_count].astype(jnp.int32)
    slot = (told[:, :top] ^ lax.axis_index("expert")) * CAP + told[:, top:]
    slot_range = jnp.arange(slots, dtype=jnp.int32)[:, None]

    def across(blocks):
        return [blocks[0]] + [
            lax.ppermute(blocks[k], "expert", [(i, i ^ k) for i in range(groups)]) for k in range(1, groups)
        ]

    def pass_on(below, above, step):
        upward = [(2 * i + c, 2 * i + 2 + c) for i in range(step - 1, planes - 1) for c in (0, 1)]
        downward = [(2 * i + 2 + c, 2 * i + c) for i in range(planes - step) for c in (0, 1)]
        return lax.ppermute(below, "dp", upward), lax.ppermute(above, "dp", downward)

    passed = [(down_local, down_local)]
    passed.append(pass_on(*passed[0], 1))

    def routed(k):
        at = jnp.arange(k * CAP, (k + 1) * CAP, dtype=jnp.int32)[:, None]
        chosen = sum((slot[:, i, None, :] == at).astype(BF16) for i in range(top))
        return jnp.einsum("dst,dtc->dsc", chosen, arrived[:, :tok_count], preferred_element_type=F32).astype(BF16)

    rows = jnp.concatenate(across([routed(k) for k in range(groups)]), axis=1)
    rows = rows.reshape(planes, 2 * slots, width)
    rows, passed[1] = lax.optimization_barrier((rows, passed[1]))

    rows = rows.reshape(planes, 2, groups, CAP, width)
    rows = [jnp.swapaxes(rows[:, :, :, low:high], 1, 2).reshape(planes, -1, width) for low, high in PARTS]
    rows = [jnp.concatenate([some, other(some)], axis=2) for some in rows]

    def together(*values):
        return lax.optimization_barrier(values)

    mid = planes // 2
    rising = plane < mid

    def product(part, target):
        return jnp.dot(take(rows[part], target % planes), in_weight, preferred_element_type=F32)

    def add_on(part, below, above, step):
        if step <= mid:
            send = product(part, jnp.where(rising, plane - step, plane + step))
            if below is not None:
                send = send + jnp.where(rising, below, above).astype(F32)
            return send.astype(BF16), send.astype(BF16)
        going_up = product(part, plane - step) + below.astype(F32)
        going_down = product(part, plane + step) + above.astype(F32)
        return going_up.astype(BF16), going_down.astype(BF16)

    def send_on(sending, step):
        upward = [(2 * i + c, 2 * i + 2 + c) for i in range(step) for c in (0, 1)]
        downward = [(2 * (planes - 1 - i) + c, 2 * (planes - 2 - i) + c) for i in range(step) for c in (0, 1)]
        if step == 1:
            both = lax.ppermute(sending[0], "dp", upward + downward)
            return both, both
        return lax.ppermute(sending[0], "dp", upward), lax.ppermute(sending[1], "dp", downward)

    sums = [(None, None) for part in PARTS]
    for step in range(1, planes):
        for part in range(len(PARTS)):
            if part == 1 and step > 1:
                rows[1], sums[1], passed[step] = together(rows[1], sums[1], passed[step])
            if part == 1 and step + 1 < planes:
                passed.append(pass_on(*passed[step], step + 1))
            sending = add_on(part, *sums[part], step)
            if part > 0:
                _, sums[part - 1] = together(sending, sums[part - 1])
            sums[part] = send_on(sending, step)
    pieces = [down_local] + [
        jnp.where(plane >= step, passed[step][0], passed[planes - step][1]) for step in range(1, planes)
    ]
    pieces = jnp.stack(pieces)
    pieces = jnp.concatenate([take(pieces, (plane - p) % planes) for p in range(planes)], axis=1)
    out_weight = [lax.dynamic_slice_in_dim(pieces, which * half, half, 0) for which in (core, 1 - core)]

    def outputs_of(part):
        below, above = sums[part]
        total = product(part, plane) + below.astype(F32) + above.astype(F32)
        hidden = (jax.nn.silu(total[:, :half]) * total[:, half:]).astype(BF16)
        ours = jnp.dot(hidden, out_weight[0], preferred_element_type=F32)
        return (ours + jnp.dot(other(hidden), out_weight[1], preferred_element_type=F32)).astype(BF16)

    coarse = lax.reduce_precision(probs, 8, 7)

    def combined(part, blocks, side):
        low, high = PARTS[part]
        size = high - low
        back = jnp.concatenate([lax.dynamic_slice_in_dim(some, side * size, size, 0) for some in blocks], axis=0)
        side_slot, side_probs, side_coarse = take(slot, 2 * plane + side), take(probs, side), take(coarse, side)
        here = jnp.concatenate([jnp.arange(k * CAP + low, k * CAP + high, dtype=jnp.int32) for k in range(groups)])
        weights = [
            sum(jnp.where(side_slot[k, :, None] == here, some[:, k, None], 0.0) for k in range(top)).astype(BF16)
            for some in (side_coarse, side_probs - side_coarse)
        ]
        both = jnp.dot(jnp.concatenate(weights, axis=0), back, preferred_element_type=F32)
        return both[:tok_count] + both[tok_count:]

    mixed = [0.0, 0.0]
    for part in range(len(PARTS)):
        outputs = outputs_of(part)
        blocks = across(split(outputs.reshape(groups, -1, outputs.shape[1])))
        if part + 1 < len(PARTS):
            blocks, sums[part + 1] = together(blocks, sums[part + 1])
        mixed = [mixed[away] + combined(part, blocks, core ^ away) for away in range(2)]
    mine, theirs = mixed[0].astype(BF16), other(mixed[1].astype(BF16))
    sides = [jnp.where(core == 0, mine, theirs), jnp.where(core == 0, theirs, mine)]
    return jnp.concatenate(
        [side[:, p * width : (p + 1) * width] for p in range(planes) for side in sides], axis=1
    )


def solution(mesh):
    placed = (
        P(("dp", "expert"), None),
        P(("dp", "expert"), None),
        P(("dp", "expert"), None),
        P("expert", "dp", None),
        P("expert", "dp", None),
        P("expert", None, "dp"),
    )
    return jax.shard_map(
        on_device, mesh=mesh, in_specs=placed, out_specs=P(("dp", "expert"), None), check_vma=False
    )
```

```python
import jax
import jax.numpy as jnp
from jax import lax
from jax.sharding import PartitionSpec as P

CAP = 80
PARTS = ((0, 40), (40, 80))
F32 = jnp.float32
BF16 = jnp.bfloat16
NOTE_ROWS = 8


def ranks_of(ids, groups):
    flat = ids.reshape(-1)
    count = flat.shape[0]
    onehot = (flat[:, None] == jnp.arange(groups, dtype=jnp.int32)).astype(BF16)
    before = (jnp.arange(count)[:, None] > jnp.arange(count)[None, :]).astype(BF16)
    ranks = jnp.dot(before, onehot, preferred_element_type=F32)
    return jnp.sum(ranks * onehot.astype(F32), axis=1).reshape(ids.shape)


def take(array, index):
    return lax.dynamic_index_in_dim(array, index, 0, keepdims=False)


def on_device(tokens, expert_ids, gate_probs, gate_weight, up_weight, down_weight):
    tok_count, model_width = tokens.shape
    top = expert_ids.shape[1]
    n_dp, groups = lax.axis_size("dp"), lax.axis_size("expert")
    planes = n_dp // 2
    place = lax.axis_index("dp")
    plane, core = place // 2, place % 2
    width = model_width // n_dp
    hidden_width = gate_weight.shape[2]
    half = hidden_width // 2
    slots = groups * CAP
    swap = [(i, i ^ 1) for i in range(n_dp)]

    def other(array):
        return lax.ppermute(array, "dp", swap)

    def columns(array, which):
        return lax.dynamic_slice_in_dim(array, which * half, half, 1)

    def split(array):
        return [take(array, which) for which in range(array.shape[0])]

    notes = jnp.concatenate([expert_ids.astype(F32).T, ranks_of(expert_ids, groups).T], axis=0)
    notes = jnp.pad(notes, ((0, NOTE_ROWS - 2 * top), (0, width - tok_count))).astype(BF16)
    sent = jnp.concatenate([tokens, jnp.tile(notes, (1, n_dp))], axis=0)
    arrived = lax.all_to_all(sent, "dp", split_axis=1, concat_axis=0, tiled=True)
    arrived = arrived.reshape(n_dp, tok_count + NOTE_ROWS, width)

    gate_local, up_local, down_local = gate_weight[0], up_weight[0], down_weight[0]
    keep = jnp.concatenate([columns(gate_local, core), columns(up_local, core)], axis=1)
    give = jnp.concatenate([columns(gate_local, 1 - core), columns(up_local, 1 - core)], axis=1)
    in_weight = jnp.concatenate([keep, other(give)], axis=0)
    other_probs = other(gate_probs)
    probs = jnp.where(core == 0, jnp.stack([gate_probs, other_probs]), jnp.stack([other_probs, gate_probs]))
    arrived, in_weight, probs = lax.optimization_barrier((arrived, in_weight, probs))

    told = arrived[:, tok_count : tok_count + 2 * top, :tok_count].astype(jnp.int32)
    slot = (told[:, :top] ^ lax.axis_index("expert")) * CAP + told[:, top:]
    slot_range = jnp.arange(slots, dtype=jnp.int32)[:, None]

    def across(blocks):
        return [blocks[0]] + [
            lax.ppermute(blocks[k], "expert", [(i, i ^ k) for i in range(groups)]) for k in range(1, groups)
        ]

    def pass_on(below, above, step):
        upward = [(2 * i + c, 2 * i + 2 + c) for i in range(step - 1, planes - 1) for c in (0, 1)]
        downward = [(2 * i + 2 + c, 2 * i + c) for i in range(planes - step) for c in (0, 1)]
        return lax.ppermute(below, "dp", upward), lax.ppermute(above, "dp", downward)

    passed = [(down_local, down_local)]
    passed.append(pass_on(*passed[0], 1))

    def routed(k):
        at = jnp.arange(k * CAP, (k + 1) * CAP, dtype=jnp.int32)[:, None]
        chosen = sum((slot[:, i, None, :] == at).astype(BF16) for i in range(top))
        return jnp.einsum("dst,dtc->dsc", chosen, arrived[:, :tok_count], preferred_element_type=F32).astype(BF16)

    rows = jnp.concatenate(across([routed(k) for k in range(groups)]), axis=1)
    rows = rows.reshape(planes, 2 * slots, width)
    rows, passed[1] = lax.optimization_barrier((rows, passed[1]))

    rows = rows.reshape(planes, 2, groups, CAP, width)
    rows = [jnp.swapaxes(rows[:, :, :, low:high], 1, 2).reshape(planes, -1, width) for low, high in PARTS]
    rows = [jnp.concatenate([some, other(some)], axis=2) for some in rows]

    def together(*values):
        return lax.optimization_barrier(values)

    mid = planes // 2
    rising = plane < mid

    def product(part, target):
        return jnp.dot(take(rows[part], target % planes), in_weight, preferred_element_type=F32)

    def add_on(part, below, above, step):
        if step <= mid:
            send = product(part, jnp.where(rising, plane - step, plane + step))
            if below is not None:
                send = send + jnp.where(rising, below, above).astype(F32)
            return send.astype(BF16), send.astype(BF16)
        going_up = product(part, plane - step) + below.astype(F32)
        going_down = product(part, plane + step) + above.astype(F32)
        return going_up.astype(BF16), going_down.astype(BF16)

    def send_on(sending, step):
        upward = [(2 * i + c, 2 * i + 2 + c) for i in range(step) for c in (0, 1)]
        downward = [(2 * (planes - 1 - i) + c, 2 * (planes - 2 - i) + c) for i in range(step) for c in (0, 1)]
        if step == 1:
            both = lax.ppermute(sending[0], "dp", upward + downward)
            return both, both
        return lax.ppermute(sending[0], "dp", upward), lax.ppermute(sending[1], "dp", downward)

    sums = [(None, None) for part in PARTS]
    for step in range(1, planes):
        for part in range(len(PARTS)):
            if part == 1 and step > 1:
                rows[1], sums[1], passed[step] = together(rows[1], sums[1], passed[step])
            if part == 1 and step + 1 < planes:
                passed.append(pass_on(*passed[step], step + 1))
            sending = add_on(part, *sums[part], step)
            if part > 0:
                _, sums[part - 1] = together(sending, sums[part - 1])
            sums[part] = send_on(sending, step)
    pieces = [down_local] + [
        jnp.where(plane >= step, passed[step][0], passed[planes - step][1]) for step in range(1, planes)
    ]
    pieces = jnp.stack(pieces)
    pieces = jnp.concatenate([take(pieces, (plane - p) % planes) for p in range(planes)], axis=1)
    out_weight = [lax.dynamic_slice_in_dim(pieces, which * half, half, 0) for which in (core, 1 - core)]

    def outputs_of(part):
        below, above = sums[part]
        total = product(part, plane) + below.astype(F32) + above.astype(F32)
        hidden = (jax.nn.silu(total[:, :half]) * total[:, half:]).astype(BF16)
        ours = jnp.dot(hidden, out_weight[0], preferred_element_type=F32)
        return (ours + jnp.dot(other(hidden), out_weight[1], preferred_element_type=F32)).astype(BF16)

    coarse = lax.reduce_precision(probs, 8, 7)

    def combined(part, blocks, side):
        low, high = PARTS[part]
        size = high - low
        back = jnp.concatenate([lax.dynamic_slice_in_dim(some, side * size, size, 0) for some in blocks], axis=0)
        side_slot, side_probs, side_coarse = take(slot, 2 * plane + side), take(probs, side), take(coarse, side)
        here = jnp.concatenate([jnp.arange(k * CAP + low, k * CAP + high, dtype=jnp.int32) for k in range(groups)])
        weights = [
            sum(jnp.where(side_slot[k, :, None] == here, some[:, k, None], 0.0) for k in range(top)).astype(BF16)
            for some in (side_coarse, side_probs - side_coarse)
        ]
        both = jnp.dot(jnp.concatenate(weights, axis=0), back, preferred_element_type=F32)
        return both[:tok_count] + both[tok_count:]

    mixed = [0.0, 0.0]
    for part in range(len(PARTS)):
        outputs = outputs_of(part)
        blocks = across(split(outputs.reshape(groups, -1, outputs.shape[1])))
        if part + 1 < len(PARTS):
            blocks[-1], sums[part + 1] = together(blocks[-1], sums[part + 1])
        mixed = [mixed[away] + combined(part, blocks, core ^ away) for away in range(2)]
    mine, theirs = mixed[0].astype(BF16), other(mixed[1].astype(BF16))
    sides = [jnp.where(core == 0, mine, theirs), jnp.where(core == 0, theirs, mine)]
    return jnp.concatenate(
        [side[:, p * width : (p + 1) * width] for p in range(planes) for side in sides], axis=1
    )


def solution(mesh):
    placed = (
        P(("dp", "expert"), None),
        P(("dp", "expert"), None),
        P(("dp", "expert"), None),
        P("expert", "dp", None),
        P("expert", "dp", None),
        P("expert", None, "dp"),
    )
    return jax.shard_map(
        on_device, mesh=mesh, in_specs=placed, out_specs=P(("dp", "expert"), None), check_vma=False
    )
```

```python
import jax
import jax.numpy as jnp
from jax import lax
from jax.sharding import PartitionSpec as P

CAP = 80
PARTS = ((0, 40), (40, 80))
F32 = jnp.float32
BF16 = jnp.bfloat16
NOTE_ROWS = 8


def ranks_of(ids, groups):
    flat = ids.T.reshape(-1)
    places = jnp.arange(flat.shape[0])
    onehot = (jnp.arange(groups, dtype=jnp.int32)[:, None] == flat[None, :]).astype(BF16)
    before = (places[:, None] < places[None, :]).astype(BF16)
    ranks = jnp.dot(onehot, before, preferred_element_type=F32)
    return jnp.sum(ranks * onehot.astype(F32), axis=0).reshape(ids.shape[1], ids.shape[0])


def take(array, index):
    return lax.dynamic_index_in_dim(array, index, 0, keepdims=False)


def on_device(tokens, expert_ids, gate_probs, gate_weight, up_weight, down_weight):
    tok_count, model_width = tokens.shape
    top = expert_ids.shape[1]
    n_dp, groups = lax.axis_size("dp"), lax.axis_size("expert")
    planes = n_dp // 2
    place = lax.axis_index("dp")
    plane, core = place // 2, place % 2
    width = model_width // n_dp
    hidden_width = gate_weight.shape[2]
    half = hidden_width // 2
    slots = groups * CAP
    swap = [(i, i ^ 1) for i in range(n_dp)]

    def other(array):
        return lax.ppermute(array, "dp", swap)

    def columns(array, which):
        return lax.dynamic_slice_in_dim(array, which * half, half, 1)

    def split(array):
        return [take(array, which) for which in range(array.shape[0])]

    notes = jnp.concatenate([expert_ids.astype(F32).T, ranks_of(expert_ids, groups)], axis=0)
    notes = jnp.pad(notes, ((0, NOTE_ROWS - 2 * top), (0, width - tok_count))).astype(BF16)
    sent = jnp.concatenate([tokens, jnp.tile(notes, (1, n_dp))], axis=0)
    arrived = lax.all_to_all(sent, "dp", split_axis=1, concat_axis=0, tiled=True)
    arrived = arrived.reshape(n_dp, tok_count + NOTE_ROWS, width)

    gate_local, up_local, down_local = gate_weight[0], up_weight[0], down_weight[0]
    keep = jnp.concatenate([columns(gate_local, core), columns(up_local, core)], axis=1)
    give = jnp.concatenate([columns(gate_local, 1 - core), columns(up_local, 1 - core)], axis=1)
    in_weight = jnp.concatenate([keep, other(give)], axis=0)
    other_probs = other(gate_probs)
    probs = jnp.where(core == 0, jnp.stack([gate_probs, other_probs]), jnp.stack([other_probs, gate_probs]))
    arrived, in_weight, probs = lax.optimization_barrier((arrived, in_weight, probs))

    told = arrived[:, tok_count : tok_count + 2 * top, :tok_count].astype(jnp.int32)
    slot = (told[:, :top] ^ lax.axis_index("expert")) * CAP + told[:, top:]
    slot_range = jnp.arange(slots, dtype=jnp.int32)[:, None]

    def across(blocks):
        return [blocks[0]] + [
            lax.ppermute(blocks[k], "expert", [(i, i ^ k) for i in range(groups)]) for k in range(1, groups)
        ]

    def pass_on(below, above, step):
        upward = [(2 * i + c, 2 * i + 2 + c) for i in range(step - 1, planes - 1) for c in (0, 1)]
        downward = [(2 * i + 2 + c, 2 * i + c) for i in range(planes - step) for c in (0, 1)]
        return lax.ppermute(below, "dp", upward), lax.ppermute(above, "dp", downward)

    passed = [(down_local, down_local)]
    passed.append(pass_on(*passed[0], 1))

    def routed(k):
        at = jnp.arange(k * CAP, (k + 1) * CAP, dtype=jnp.int32)[:, None]
        chosen = sum((slot[:, i, None, :] == at).astype(BF16) for i in range(top))
        return jnp.einsum("dst,dtc->dsc", chosen, arrived[:, :tok_count], preferred_element_type=F32).astype(BF16)

    rows = jnp.concatenate(across([routed(k) for k in range(groups)]), axis=1)
    rows = rows.reshape(planes, 2 * slots, width)
    rows, passed[1] = lax.optimization_barrier((rows, passed[1]))

    rows = rows.reshape(planes, 2, groups, CAP, width)
    rows = [jnp.swapaxes(rows[:, :, :, low:high], 1, 2).reshape(planes, -1, width) for low, high in PARTS]
    rows = [jnp.concatenate([some, other(some)], axis=2) for some in rows]

    def together(*values):
        return lax.optimization_barrier(values)

    mid = planes // 2
    rising = plane < mid

    def product(part, target):
        return jnp.dot(take(rows[part], target % planes), in_weight, preferred_element_type=F32)

    def add_on(part, below, above, step):
        if step <= mid:
            send = product(part, jnp.where(rising, plane - step, plane + step))
            if below is not None:
                send = send + jnp.where(rising, below, above).astype(F32)
            return send.astype(BF16), send.astype(BF16)
        going_up = product(part, plane - step) + below.astype(F32)
        going_down = product(part, plane + step) + above.astype(F32)
        return going_up.astype(BF16), going_down.astype(BF16)

    def send_on(sending, step):
        upward = [(2 * i + c, 2 * i + 2 + c) for i in range(step) for c in (0, 1)]
        downward = [(2 * (planes - 1 - i) + c, 2 * (planes - 2 - i) + c) for i in range(step) for c in (0, 1)]
        if step == 1:
            both = lax.ppermute(sending[0], "dp", upward + downward)
            return both, both
        return lax.ppermute(sending[0], "dp", upward), lax.ppermute(sending[1], "dp", downward)

    sums = [(None, None) for part in PARTS]
    for step in range(1, planes):
        for part in range(len(PARTS)):
            if part == 1 and step > 1:
                rows[1], sums[1], passed[step] = together(rows[1], sums[1], passed[step])
            if part == 1 and step + 1 < planes:
                passed.append(pass_on(*passed[step], step + 1))
            sending = add_on(part, *sums[part], step)
            if part > 0:
                _, sums[part - 1] = together(sending, sums[part - 1])
            sums[part] = send_on(sending, step)
    pieces = [down_local] + [
        jnp.where(plane >= step, passed[step][0], passed[planes - step][1]) for step in range(1, planes)
    ]
    pieces = jnp.stack(pieces)
    pieces = jnp.concatenate([take(pieces, (plane - p) % planes) for p in range(planes)], axis=1)
    out_weight = [lax.dynamic_slice_in_dim(pieces, which * half, half, 0) for which in (core, 1 - core)]

    def outputs_of(part):
        below, above = sums[part]
        total = lax.optimization_barrier(product(part, plane)) + below.astype(F32) + above.astype(F32)
        hidden = (jax.nn.silu(total[:, :half]) * total[:, half:]).astype(BF16)
        ours = jnp.dot(hidden, out_weight[0], preferred_element_type=F32)
        return (ours + jnp.dot(other(hidden), out_weight[1], preferred_element_type=F32)).astype(BF16)

    coarse = lax.reduce_precision(probs, 8, 7)

    def combined(part, blocks, side):
        low, high = PARTS[part]
        size = high - low
        back = jnp.concatenate([lax.dynamic_slice_in_dim(some, side * size, size, 0) for some in blocks], axis=0)
        side_slot, side_probs, side_coarse = take(slot, 2 * plane + side), take(probs, side), take(coarse, side)
        here = jnp.concatenate([jnp.arange(k * CAP + low, k * CAP + high, dtype=jnp.int32) for k in range(groups)])
        weights = [
            sum(jnp.where(side_slot[k, :, None] == here, some[:, k, None], 0.0) for k in range(top)).astype(BF16)
            for some in (side_coarse, side_probs - side_coarse)
        ]
        both = jnp.dot(jnp.concatenate(weights, axis=0), back, preferred_element_type=F32)
        return both[:tok_count] + both[tok_count:]

    mixed = [0.0, 0.0]
    for part in range(len(PARTS)):
        outputs = outputs_of(part)
        blocks = across(split(outputs.reshape(groups, -1, outputs.shape[1])))
        if part + 1 < len(PARTS):
            blocks[-1], sums[part + 1] = together(blocks[-1], sums[part + 1])
        mixed = [mixed[away] + combined(part, blocks, core ^ away) for away in range(2)]
    mine, theirs = mixed[0].astype(BF16), other(mixed[1].astype(BF16))
    sides = [jnp.where(core == 0, mine, theirs), jnp.where(core == 0, theirs, mine)]
    return jnp.concatenate(
        [side[:, p * width : (p + 1) * width] for p in range(planes) for side in sides], axis=1
    )


def solution(mesh):
    placed = (
        P(("dp", "expert"), None),
        P(("dp", "expert"), None),
        P(("dp", "expert"), None),
        P("expert", "dp", None),
        P("expert", "dp", None),
        P("expert", None, "dp"),
    )
    return jax.shard_map(
        on_device, mesh=mesh, in_specs=placed, out_specs=P(("dp", "expert"), None), check_vma=False
    )
```
